32 devices in a mesh: seq: 8 (over y, x, core), tp: 4 (over z).
Axes of the slice: x: 2, y: 2, z: 4, core: 2. Of those that a mesh axis runs over, the one named last changes fastest.
Arguments:
- queries: bfloat16 [4096, 6144], P('seq', 'tp'), may hold values from -6 to 6
- keys: bfloat16 [4096, 1024], P('seq', 'tp'), may hold values from -6 to 6
- values: bfloat16 [4096, 1024], P('seq', 'tp'), may hold values from -6 to 6
- segment_ids: int32 [4096], replicated, may hold values from 0 to 3, never falling along the last dimension, each value on 1 to 3072 neighbouring positions
- packing: int32 [32, 2], replicated, may hold values from 0 to 7, as said below
- out_weight: bfloat16 [6144, 12288], P('tp', 'seq'), may hold values from -0.625 to 0.625
Outputs:
- attended: bfloat16 [4096, 12288], P('seq', 'tp')
The draws below stay inside these ranges and needn't reach their ends.
Inputs may be any that keep to these rules, and one draw needn't show every extreme that they name: `packing`: each arriving block gets a distinct packed place, so every packed shard receives exactly 4 blocks at offsets 0 to 3; the blocks of one shard go to 4 different packed shards. `segment_ids`: document ids never fall along the tokens; each document has 1 to 3072 tokens and one has exactly 3072.
All inputs are finite; a program needn't handle non-finite values.
Results may differ from the reference program's by a relative error of at most 0.015.
Values may be sent and summed in bfloat16 or wider, within the bound.
No kernel may reach another device: no remote copies, remote signals or barrier semaphores. Data moves between devices by JAX's collectives and lax.ppermute only.
A program may use at most 128 MiB of HBM per device.

```python
import math
import jax
import jax.numpy as jnp
import numpy as np
from jax import lax

D = 12288
HEAD_DIM = 128
KV_HEADS = 8
HEADS = 48
WINDOW = 4096
BLOCK = 128
TOK_DEV = 512
TOKENS = 4096
HD = 6144
KVD = 1024
BPD = 4
NBLK = 32
DOCS = 4
DOC_MOST = 3072
N_TP = 4


def draw_queries(key, part):
    base = jnp.clip(1.41 * jax.random.normal(jax.random.fold_in(key, 1), (TOKENS, HD), jnp.float32), -6.0, 6.0)
    return base.astype(jnp.bfloat16)


def draw_keys(key, part):
    base = jnp.clip(1.41 * jax.random.normal(jax.random.fold_in(key, 2), (TOKENS, KVD), jnp.float32), -6.0, 6.0)
    return base.astype(jnp.bfloat16)


def draw_packing(key, part):
    shard_count = NBLK // BPD
    key_place, key_shift, key_order, key_offset = jax.random.split(jax.random.fold_in(key, 11), 4)
    placed = jax.random.permutation(key_place, shard_count).astype(jnp.int32)
    shifts = jax.random.permutation(key_shift, shard_count)[:BPD].astype(jnp.int32)
    tie_break = jnp.arange(BPD, dtype=jnp.int32)[None, :]
    slot_order = jnp.argsort(jax.random.randint(key_order, (shard_count, BPD), 0, 4096) * BPD + tie_break, axis=1).astype(jnp.int32)
    target_shard = (placed[:, None] + shifts[slot_order]) % shard_count
    offset_table = jnp.argsort(jax.random.randint(key_offset, (shard_count, BPD), 0, 4096) * BPD + tie_break, axis=1).astype(jnp.int32)
    target_offset = offset_table[target_shard, slot_order]
    return jnp.stack([target_shard.reshape(-1), target_offset.reshape(-1)], axis=1).astype(jnp.int32)


def raised(values, key, source, target, shards_of, factor):
    def block_of(dim):
        return (jnp.arange(values.shape[dim]) // (values.shape[dim] // shards_of)).reshape((-1,) + (1,) * (values.ndim - 1 - dim))

    first = jax.random.permutation(key, shards_of)[block_of(target)]
    second = (block_of(target) + shards_of // 2) % shards_of
    return jnp.where((block_of(source) == first) | (block_of(source) == second), factor * values, values)


def shard_levels(stream_key, shape, cuts, smallest, top_value):
    factor_of, own = 1.0, jax.random.fold_in(stream_key, 6)
    for dim, shards_of in cuts:
        steps = jnp.exp(jax.random.uniform(jax.random.fold_in(own, dim), (shards_of,), jnp.float32, smallest / len(cuts), top_value / len(cuts)))
        factor_of = factor_of * jnp.repeat(steps, shape[dim] // shards_of).reshape([-1 if axis == dim else 1 for axis in range(len(shape))])
    return factor_of


def profile(count, total, bound, slope):
    portions = [(1 << 20) // math.isqrt(standing ** slope) + 1 for standing in range(2, count + 1)]
    spare, counts = total - bound - (count - 1), [1] * (count - 1)
    while spare > 0:
        movable = [i for i in range(count - 1) if counts[i] < bound]
        pool, budget = sum([portions[i] for i in movable]), spare
        for i in movable:
            extra = min(bound - counts[i], max(1, budget * portions[i] // pool), spare)
            counts[i] = counts[i] + extra
            spare = spare - extra
    return np.array([bound] + counts)


def ragged_sizes(stream_key, number_of, total, bound, skew):
    if number_of == 2:
        one = jax.random.randint(stream_key, (), max(1, total - bound), min(bound, total - 1) + 1)
        return jnp.stack([one, total - one])
    lengths = jnp.asarray(profile(number_of, total, bound, skew), jnp.int32)
    twos = (number_of - 1) // 2
    giver, taker = lengths[1:1 + 2 * twos:2], lengths[2:2 + 2 * twos:2]
    margin = jnp.minimum(giver - 1, bound - taker)
    moved = jax.random.randint(jax.random.fold_in(stream_key, 1), (twos,), 0, 1 << 20) % (margin + 1)
    lengths = lengths.at[1:1 + 2 * twos:2].set(giver - moved).at[2:2 + 2 * twos:2].set(taker + moved)
    return lengths[jax.random.permutation(jax.random.fold_in(stream_key, 2), number_of)]


def scatter_about(rng, dims, scale, reach, cuts=(), kind=jnp.bfloat16):
    values = scale * jax.random.normal(rng, dims, jnp.float32)
    if cuts:
        values = values * shard_levels(rng, dims, cuts, -0.22, 0.18)
    return jnp.clip(values, -reach, reach).astype(kind)


def noise_with(stream_key, dims, width, bound, shards, heavy, held_as=jnp.bfloat16):
    entries = width * jax.random.normal(stream_key, dims, jnp.float32)
    if shards:
        entries = entries * shard_levels(stream_key, dims, shards, -0.22, 0.18)
    return jnp.clip(raised(entries, jax.random.fold_in(stream_key, 3), *heavy), -bound, bound).astype(held_as)


def setup_inputs(seed: int = 0) -> dict:
    streams_of = jax.random.split(jax.random.key(seed), 7)
    return {
        "queries": draw_queries(jax.random.fold_in(streams_of[6], 71), 0),
        "keys": draw_keys(jax.random.fold_in(streams_of[6], 71), 0),
        "values": scatter_about(streams_of[2], (TOKENS, KVD), 1.0, 6.0, ((0, 8), (1, 4))),
        "segment_ids": jnp.searchsorted(jnp.cumsum(ragged_sizes(streams_of[3], DOCS, TOKENS, DOC_MOST, 2)), jnp.arange(TOKENS), side="right").astype(jnp.int32),
        "packing": draw_packing(jax.random.fold_in(streams_of[6], 71), 0),
        "out_weight": noise_with(streams_of[5], (HD, D), (HD // 32) ** -0.5, 0.625, ((0, 4), (1, 8)), (0, 1, 8, 2.0)),
    }


def attend_head(q_rows, k_rows, v_rows, q_pos, k_pos, q_seg, k_seg):
    scores = lax.dot_general(q_rows, k_rows, (((1,), (1,)), ((), ())), preferred_element_type=jnp.float32)
    scores = scores * (1.0 / math.sqrt(HEAD_DIM))
    allowed = (k_pos[None, :] <= q_pos[:, None]) & (k_pos[None, :] > q_pos[:, None] - WINDOW)
    allowed = allowed & (k_seg[None, :] == q_seg[:, None])
    scores = jnp.where(allowed, scores, -jnp.inf)
    top_score = lax.optimization_barrier(jnp.max(scores, axis=1, keepdims=True))
    expo = jnp.exp(scores - top_score)
    weights = (expo / lax.optimization_barrier(jnp.sum(expo, axis=1, keepdims=True))).astype(jnp.bfloat16)
    return jnp.dot(weights, v_rows, preferred_element_type=jnp.float32).astype(jnp.bfloat16)

def reference(queries, keys, values, segment_ids, packing, out_weight):
    target = packing[:, 0] * BPD + packing[:, 1]
    source = jnp.zeros((NBLK,), jnp.int32).at[target].set(jnp.arange(NBLK, dtype=jnp.int32))

    def repack(array):
        return array.reshape(NBLK, BLOCK, array.shape[1])[source].reshape(TOKENS, array.shape[1])
    packed_q = repack(queries)
    packed_k = repack(keys)
    packed_v = repack(values)
    group_size = HEADS // KV_HEADS
    padded_k = jnp.concatenate([jnp.zeros((WINDOW, KVD), jnp.bfloat16), packed_k], axis=0)
    padded_v = jnp.concatenate([jnp.zeros((WINDOW, KVD), jnp.bfloat16), packed_v], axis=0)
    padded_seg = jnp.concatenate([jnp.full((WINDOW,), -1, jnp.int32), segment_ids], axis=0)

    def one_block(block_index):
        first_row = (block_index * TOK_DEV).astype(jnp.int32)
        q_block = lax.dynamic_slice_in_dim(packed_q, first_row, TOK_DEV, 0)
        k_block = lax.dynamic_slice_in_dim(padded_k, first_row, WINDOW + TOK_DEV, 0)
        v_block = lax.dynamic_slice_in_dim(padded_v, first_row, WINDOW + TOK_DEV, 0)
        q_pos = first_row + jnp.arange(TOK_DEV, dtype=jnp.int32)
        k_pos = first_row - WINDOW + jnp.arange(WINDOW + TOK_DEV, dtype=jnp.int32)
        q_seg = lax.dynamic_slice_in_dim(segment_ids, first_row, TOK_DEV, 0)
        k_seg = lax.dynamic_slice_in_dim(padded_seg, first_row, WINDOW + TOK_DEV, 0)

        def one_head(head_index):
            q_head = lax.dynamic_slice_in_dim(q_block, head_index * HEAD_DIM, HEAD_DIM, 1)
            kv_start = head_index // group_size * HEAD_DIM
            k_head = lax.dynamic_slice_in_dim(k_block, kv_start, HEAD_DIM, 1)
            v_head = lax.dynamic_slice_in_dim(v_block, kv_start, HEAD_DIM, 1)
            return attend_head(q_head, k_head, v_head, q_pos, k_pos, q_seg, k_seg)
        per_head = lax.map(one_head, jnp.arange(HEADS, dtype=jnp.int32))
        return jnp.transpose(per_head, (1, 0, 2)).reshape(TOK_DEV, HD)
    heads_out = lax.map(one_block, jnp.arange(TOKENS // TOK_DEV, dtype=jnp.int32)).reshape(TOKENS, HD)
    group_rows = HD // N_TP

    def add_group(group_index, running):
        first_col = (group_index * group_rows).astype(jnp.int32)
        part_cols = lax.dynamic_slice_in_dim(heads_out, first_col, group_rows, 1)
        part_rows = lax.dynamic_slice_in_dim(out_weight, first_col, group_rows, 0)
        partial_sum = jnp.dot(part_cols, part_rows, preferred_element_type=jnp.float32)
        rounded = lax.optimization_barrier(partial_sum.astype(jnp.bfloat16))
        return running + rounded.astype(jnp.float32)
    total = lax.fori_loop(0, N_TP, add_group, jnp.zeros((TOKENS, D), jnp.float32))
    return total.astype(jnp.bfloat16)
```

```python
import functools
import math

import jax
import jax.numpy as jnp
from jax import lax
from jax.experimental import pallas as pl
from jax.experimental.pallas import tpu as pltpu
from jax.sharding import PartitionSpec as P

HEAD_DIM = 128
WINDOW = 4096
BLOCK = 128
KEY_TILE = 512
MASKED = -1e30
SCALE = math.log2(math.e) / math.sqrt(HEAD_DIM)


def attention_kernel(group, kv_heads, n_kv, place, low, rows_at, q_ref, qseg_ref, seg_ref, *refs):
    kv_refs, out_ref, packed_kv = refs[:n_kv], refs[n_kv], refs[n_kv + 1]
    step = pl.program_id(0)
    kv_rows = kv_refs[0].shape[0]

    @pl.when(step == 0)
    def _():
        def move(block, _):
            row = rows_at[block]
            for i, kv_ref in enumerate(kv_refs):

                @pl.when((row >= i * kv_rows) & (row < (i + 1) * kv_rows))
                def _(i=i, kv_ref=kv_ref):
                    at = pl.multiple_of(row - i * kv_rows, BLOCK)
                    packed_kv[pl.ds(pl.multiple_of(block * BLOCK, BLOCK), BLOCK), :] = kv_ref[pl.ds(at, BLOCK), :]

            return 0

        lax.fori_loop(0, rows_at.shape[0], move, 0)

    first = place[step] * BLOCK
    q_pos = first + lax.broadcasted_iota(jnp.int32, (BLOCK, KEY_TILE), 0)
    q_seg = qseg_ref[...]
    lo_tile = low[step] // KEY_TILE
    hi_tile = (first + BLOCK - 1) // KEY_TILE + 1
    kv_cols = kv_heads * HEAD_DIM

    for kv_head in range(kv_heads):
        q = jnp.concatenate(
            [q_ref[:, (kv_head * group + h) * HEAD_DIM : (kv_head * group + h + 1) * HEAD_DIM] for h in range(group)],
            axis=0,
        )
        q = (q.astype(jnp.float32) * SCALE).astype(jnp.bfloat16)

        def tile(t, carry, q=q, kv_head=kv_head):
            top, total, acc = carry
            rows = pl.ds(pl.multiple_of(t * KEY_TILE, KEY_TILE), KEY_TILE)
            keys = packed_kv[rows, kv_head * HEAD_DIM : (kv_head + 1) * HEAD_DIM]
            values = packed_kv[rows, kv_cols + kv_head * HEAD_DIM : kv_cols + (kv_head + 1) * HEAD_DIM]
            k_pos = t * KEY_TILE + lax.broadcasted_iota(jnp.int32, (BLOCK, KEY_TILE), 1)
            kept = (k_pos <= q_pos) & (k_pos > q_pos - WINDOW) & (seg_ref[:, rows] == q_seg)
            scores = lax.dot_general(q, keys, (((1,), (1,)), ((), ())), preferred_element_type=jnp.float32)
            scores = jnp.where(kept[None], scores.reshape(group, BLOCK, KEY_TILE), MASKED)
            scores = scores.reshape(group * BLOCK, KEY_TILE)
            new_top = jnp.maximum(top, jnp.max(scores, axis=1, keepdims=True))
            expo = jnp.exp2(scores - new_top)
            keep = jnp.exp2(top - new_top)
            total = total * keep + jnp.sum(expo, axis=1, keepdims=True)
            acc = acc * keep + jnp.dot(expo.astype(jnp.bfloat16), values, preferred_element_type=jnp.float32)
            return new_top, total, acc

        rows = group * BLOCK
        start = (
            jnp.full((rows, 1), MASKED, jnp.float32),
            jnp.zeros((rows, 1), jnp.float32),
            jnp.zeros((rows, HEAD_DIM), jnp.float32),
        )
        _, total, acc = lax.fori_loop(lo_tile, hi_tile, tile, start)
        heads = (acc / total).astype(jnp.bfloat16)
        for h in range(group):
            at = (kv_head * group + h) * HEAD_DIM
            out_ref[:, at : at + HEAD_DIM] = heads[h * BLOCK : (h + 1) * BLOCK]


def attend(q, kv, rows_at, place, segment_ids, first=0):
    blocks = place.shape[0]
    tokens = segment_ids.shape[0]
    kv_heads = kv[0].shape[1] // (2 * HEAD_DIM)
    group = q.shape[1] // HEAD_DIM // kv_heads
    q_seg = segment_ids.reshape(-1, BLOCK)[place]
    doc_first = jnp.sum((segment_ids[None, :] < q_seg[:, :1]).astype(jnp.int32), axis=1)
    low = jnp.maximum(doc_first, place * BLOCK - (WINDOW - 1))
    grid = pltpu.PrefetchScalarGridSpec(
        num_scalar_prefetch=3,
        grid=(blocks,),
        in_specs=[
            pl.BlockSpec((BLOCK, q.shape[1]), lambda i, *_: (first + i, 0)),
            pl.BlockSpec((BLOCK, 1), lambda i, *_: (i, 0)),
            pl.BlockSpec((1, tokens), lambda i, *_: (0, 0)),
        ]
        + [pl.BlockSpec(part.shape, lambda i, *_: (0, 0)) for part in kv],
        out_specs=pl.BlockSpec((BLOCK, q.shape[1]), lambda i, *_: (i, 0)),
        scratch_shapes=[pltpu.VMEM((tokens, kv[0].shape[1]), jnp.bfloat16)],
    )
    rows = blocks * BLOCK
    return pl.pallas_call(
        functools.partial(attention_kernel, group, kv_heads, len(kv)),
        grid_spec=grid,
        out_shape=jax.ShapeDtypeStruct((rows, q.shape[1]), jnp.bfloat16),
        compiler_params=pltpu.CompilerParams(vmem_limit_bytes=48 << 20),
        cost_estimate=pl.CostEstimate(
            flops=4 * rows * q.shape[1] * tokens // 2,
            bytes_accessed=4 * rows * q.shape[1] + 2 * tokens * kv[0].shape[1],
            transcendentals=rows * (q.shape[1] // HEAD_DIM) * tokens // 2,
        ),
        name="attend",
    )(place, low, rows_at, q, q_seg.reshape(-1, 1), segment_ids.reshape(1, -1), *kv)


def product_kernel(layout, slots, *refs):
    del slots
    out_ref = refs[-1]
    row = 0
    for h, w, adds in layout:
        total = jnp.dot(refs[h][...], refs[w][...], preferred_element_type=jnp.float32)
        for a in adds:
            total = total + refs[a][...].astype(jnp.float32)
        rows = total.shape[0]
        out_ref[row : row + rows, :] = total.astype(out_ref.dtype)
        row += rows


def product(parts, weight, slots, adds=None, tile=384, first=0, tiles=None):
    depth, cols = weight.shape[1:]
    per_group = cols // tile
    tiles = tiles or per_group
    operands = [weight]
    in_specs = [pl.BlockSpec((None, depth, tile), lambda g, j, s: (s[g], 0, first + j))]
    layout = []
    for p, h in enumerate(parts):
        rows = h.shape[0]
        operands.append(h)
        in_specs.append(pl.BlockSpec((rows, depth), lambda g, j, s: (0, 0)))
        at, more = len(operands) - 1, []
        for a, r, slotted in adds[p] if adds else ():
            operands.append(a)
            if slotted:
                in_specs.append(pl.BlockSpec((rows, tile), lambda g, j, s, r=r: (r, s[g] * per_group + first + j)))
            else:
                in_specs.append(pl.BlockSpec((rows, tile), lambda g, j, s, r=r: (r, g * tiles + j)))
            more.append(len(operands) - 1)
        layout.append((at, 0, more))
    rows = sum(h.shape[0] for h in parts)
    groups = slots.shape[0]
    return pl.pallas_call(
        functools.partial(product_kernel, layout),
        grid_spec=pltpu.PrefetchScalarGridSpec(
            num_scalar_prefetch=1,
            grid=(groups, tiles),
            in_specs=in_specs,
            out_specs=pl.BlockSpec((rows, tile), lambda g, j, s: (0, g * tiles + j)),
        ),
        out_shape=jax.ShapeDtypeStruct((rows, groups * tiles * tile), jnp.bfloat16),
        compiler_params=pltpu.CompilerParams(vmem_limit_bytes=40 << 20),
        cost_estimate=pl.CostEstimate(
            flops=2 * rows * depth * groups * tiles * tile,
            bytes_accessed=2 * depth * (rows + groups * tiles * tile) + 4 * rows * groups * tiles * tile,
            transcendentals=0,
        ),
        name="product",
    )(slots, *operands)


def pick_kernel(pools, source, *refs):
    outs = refs[pools:]
    per_out = outs[0].shape[0] // BLOCK
    for i in range(source.shape[0]):
        row = source[i] * BLOCK
        out = outs[i // per_out]
        to = slice(i % per_out * BLOCK, (i % per_out + 1) * BLOCK)
        low = 0
        for pool in refs[:pools]:

            @pl.when((row >= low) & (row < low + pool.shape[0]))
            def _(pool=pool, row=row, out=out, to=to, low=low):
                out[to, :] = pool[pl.ds(pl.multiple_of(row - low, BLOCK), BLOCK), :]

            low += pool.shape[0]


def pick_blocks(pools, cols, source, outs):
    rows = source.shape[0] * BLOCK // outs
    size = 2 * cols * (sum(p.shape[0] for p, _ in pools) + rows * outs)
    return pl.pallas_call(
        functools.partial(pick_kernel, len(pools)),
        grid_spec=pltpu.PrefetchScalarGridSpec(
            num_scalar_prefetch=1,
            grid=(1,),
            in_specs=[pl.BlockSpec((p.shape[0], cols), lambda i, s, g=g: (0, g)) for p, g in pools],
            out_specs=[pl.BlockSpec((rows, cols), lambda i, s: (0, 0))] * outs,
        ),
        out_shape=[jax.ShapeDtypeStruct((rows, cols), jnp.bfloat16)] * outs,
        compiler_params=pltpu.CompilerParams(vmem_limit_bytes=40 << 20),
        cost_estimate=pl.CostEstimate(flops=0, bytes_accessed=size, transcendentals=0),
        name="pick_blocks",
    )(source, *[p for p, _ in pools])


def sources_of(packing, per_shard):
    blocks = packing.shape[0]
    target = packing[:, 0] * per_shard + packing[:, 1]
    at = jnp.arange(blocks, dtype=jnp.int32)
    return target, jnp.sum(jnp.where(target[None, :] == at[:, None], at[None, :], 0), axis=1)


def plain_plan(queries, keys, values, segment_ids, packing, out_weight):
    tok_rows = queries.shape[0]
    per_shard = tok_rows // BLOCK
    me = lax.axis_index("seq")
    target, source = sources_of(packing, per_shard)
    place = lax.dynamic_slice_in_dim(target, me * per_shard, per_shard, 0)
    kv = lax.all_gather(jnp.concatenate([keys, values], axis=1), "seq", axis=0, tiled=True)
    heads = attend(queries, [kv], source * BLOCK, place, segment_ids)
    heads = lax.all_gather(heads, "seq", axis=0, tiled=True)
    own = lax.dynamic_slice_in_dim(source, me * per_shard, per_shard, 0)
    heads = heads.reshape(-1, BLOCK, heads.shape[1])[own].reshape(tok_rows, -1)
    weight = lax.all_gather(out_weight, "seq", axis=1, tiled=True)
    terms = jnp.dot(heads, weight, preferred_element_type=jnp.float32).astype(jnp.bfloat16)
    return lax.psum_scatter(terms, "tp", scatter_dimension=1, tiled=True)


def after(array, *others):
    return lax.optimization_barrier((array, *others))[0]


def paired_plan(queries, keys, values, segment_ids, packing, out_weight):
    tok_rows, q_cols = queries.shape
    per_shard = tok_rows // BLOCK
    quarter = out_weight.shape[1] // 2
    half = quarter // 2
    me, z = lax.axis_index("seq"), lax.axis_index("tp")
    chip, core = me // 2, me % 2
    x, pair = chip % 2, z // 2
    target, source = sources_of(packing, per_shard)
    place = lax.dynamic_slice_in_dim(target, me * per_shard, per_shard, 0)

    def across(array, mask):
        return lax.ppermute(array, "seq", [(i, i ^ mask) for i in range(8)])

    def along(array, *route):
        return lax.ppermute(array, "tp", route)

    kv = jnp.concatenate([keys, values], axis=1)
    kv_x, kv_y, kv_d = across(kv, 2), across(kv, 4), across(kv, 6)
    pieces = [lax.dynamic_slice_in_dim(out_weight, (x ^ flip) * quarter, quarter, 1) for flip in range(2)]
    kv_own = jnp.concatenate([kv, after(kv_x, *pieces), kv_y, kv_d], axis=0)
    kv_other = across(kv_own, 1)

    def row_of(block):
        relative = (block // per_shard) ^ me
        return ((relative >> 1) + 4 * (relative & 1)) * tok_rows + block % per_shard * BLOCK

    weights = []
    for flip, piece in enumerate(pieces):
        route = []
        for s in range(8):
            sy, sx, sa = s // 4, s // 2 % 2, s % 2
            d = 4 * sa + 2 * (sx ^ flip) + sy
            if s != d:
                route.append((s, d))
        weights.append(lax.ppermute(after(piece, kv_x, kv_y, kv_d), "seq", route))
    weights[0] = jnp.where(core == chip // 2, pieces[0], weights[0])

    heads = attend(queries, [kv_own, kv_other], row_of(source), place, segment_ids)
    mine = [heads, across(heads, 2), across(heads, 4)]

    weights = [(own, across(after(own, heads), 1)) for own in weights]

    here = core == pair
    near = jnp.stack([jnp.where(here, own, other) for own, other in weights])
    far = [jnp.where(here, other, own)[None] for own, other in weights]
    both = jnp.concatenate(far, axis=0)
    first, flips = jnp.zeros((1,), jnp.int32), jnp.arange(2, dtype=jnp.int32)

    def add(a, b):
        return (a.astype(jnp.float32) + b.astype(jnp.float32)).astype(jnp.bfloat16)

    shares = [(0, far[0]), (0, far[1]), (1, both), (2, both), (3, both)]
    inward, sums, arrived = [], [], []
    for i, (r, w) in enumerate(shares):
        if i == 2:
            mine.append(across(after(heads, shares[1], mine[1], mine[2]), 6))
        rows = mine[r]
        if i == 1:
            rows = after(rows, shares[0])
        elif i:
            rows = after(rows, shares[i - 1], sums[i - 2], *arrived[: i - 2])
        shares[i] = product([rows], w, first if i < 2 else flips)
        inward.append(along(shares[i], (0, 1), (3, 2)))
        sums.append(add(shares[i], inward[i]))
        arrived.append(along(sums[i], (1, 2), (2, 1)))

    own_slot = ((z & 1) ^ x).astype(jnp.int32)[None]

    near_adds = [jnp.concatenate(arrived[:2], axis=1), *arrived[2:]]

    def swap(r, first=0, tiles=2):
        share = product([mine[r]], near, 1 - own_slot, [[(near_adds[r], 0, True)]], half, first, tiles)
        return along(share, (0, 1), (1, 0), (2, 3), (3, 2))

    def total(parts, swapped, first=0, tiles=2):
        adds = [[(near_adds[r], 0, True), (some, 0, False)] for r, some in zip(parts, swapped)]
        return product([mine[r] for r in parts], near, own_slot, adds, half, first, tiles)

    early = [swap(r) for r in range(3)]
    late = [swap(3, h, 1) for h in range(2)]
    done = total((0, 1, 2), early)
    done = [done, across(done, 1)]

    picks = []
    for r in range(4):
        blocks = lax.dynamic_slice_in_dim(source, (me ^ (2 * r)) * per_shard, per_shard, 0)
        picks.append(row_of(blocks) // BLOCK)
    picks = jnp.concatenate(picks)
    result = jnp.zeros((tok_rows, 4 * quarter), jnp.bfloat16)
    for h in range(2):
        last = total((3,), [late[h]], h, 1)
        rows = pick_blocks([(done[0], h), (last, 0), (done[1], h), (across(last, 1), 0)], half, picks, 4)
        for r in range(4):
            some = across(rows[r], 2 * r) if r else rows[r]
            result = lax.dynamic_update_slice_in_dim(result, some, (chip ^ r) * quarter + h * half, 1)
    return result


def solution(mesh):
    in_specs = (P("seq", "tp"), P("seq", "tp"), P("seq", "tp"), P(), P(), P("tp", "seq"))
    out_specs = P("seq", "tp")
    paired = mesh.shape["seq"] == 8 and mesh.shape["tp"] == 4
    shards = paired_plan if paired else plain_plan
    return jax.shard_map(shards, mesh=mesh, in_specs=in_specs, out_specs=out_specs, check_vma=False)
```

```python
import functools
import math
import jax
import jax.numpy as jnp
from jax import lax
from jax.experimental import pallas as pl
from jax.experimental.pallas import tpu as pltpu
from jax.sharding import PartitionSpec as P
HEAD_DIM = 128
WINDOW = 4096
BLOCK = 128
KEY_TILE = 512
MASKED = -1e+30
SCALE = math.log2(math.e) / math.sqrt(HEAD_DIM)

def attention_kernel(group, kv_heads, n_kv, place, low, high, rows_at, q_ref, qseg_ref, seg_ref, *refs):
    kv_refs, (out_ref, packed_kv, score_ref, top_ref, total_ref, acc_ref) = (refs[:n_kv], refs[n_kv:])
    step = pl.program_id(0)
    kv_rows = kv_refs[0].shape[0]

    @pl.when(step == 0)
    def _():

        def move(block, _):
            row = rows_at[block]
            for i, kv_ref in enumerate(kv_refs):

                @pl.when((row >= i * kv_rows) & (row < (i + 1) * kv_rows))
                def _(i=i, kv_ref=kv_ref):
                    at = pl.multiple_of(row - i * kv_rows, BLOCK)
                    packed_kv[pl.ds(pl.multiple_of(block * BLOCK, BLOCK), BLOCK), :] = kv_ref[pl.ds(at, BLOCK), :]
            return 0
        lax.fori_loop(0, rows_at.shape[0], move, 0)
    first = place[step] * BLOCK
    q_pos = first + lax.broadcasted_iota(jnp.int32, (BLOCK, KEY_TILE), 0)
    q_seg = qseg_ref[...]
    lo_tile = low[step] // KEY_TILE
    hi_tile = (first + BLOCK - 1) // KEY_TILE + 1
    inner_lo = jnp.minimum((high[step] + KEY_TILE - 1) // KEY_TILE, hi_tile - 1)
    inner_hi = jnp.maximum((first + 1) // KEY_TILE, inner_lo)
    kv_cols = kv_heads * HEAD_DIM
    rows = group * BLOCK
    lanes = [slice(i * HEAD_DIM, (i + 1) * HEAD_DIM) for i in range(KEY_TILE // HEAD_DIM)]
    for kv_head in range(kv_heads):
        q = jnp.concatenate([q_ref[:, (kv_head * group + h) * HEAD_DIM:(kv_head * group + h + 1) * HEAD_DIM] for h in range(group)], axis=0)
        q = (q.astype(jnp.float32) * SCALE).astype(jnp.bfloat16)
        top_ref[...] = jnp.full((rows, HEAD_DIM), MASKED, jnp.float32)

        def score(t, _, masked, q=q, kv_head=kv_head):
            at = pl.ds(pl.multiple_of(t * KEY_TILE, KEY_TILE), KEY_TILE)
            keys = packed_kv[at, kv_head * HEAD_DIM:(kv_head + 1) * HEAD_DIM]
            scores = lax.dot_general(q, keys, (((1,), (1,)), ((), ())), preferred_element_type=jnp.float32)
            if masked:
                k_pos = t * KEY_TILE + lax.broadcasted_iota(jnp.int32, (BLOCK, KEY_TILE), 1)
                kept = (k_pos <= q_pos) & (k_pos > q_pos - WINDOW) & (seg_ref[:, at] == q_seg)
                scores = jnp.where(kept[None], scores.reshape(group, BLOCK, KEY_TILE), MASKED)
                scores = scores.reshape(rows, KEY_TILE)
            score_ref[t - lo_tile] = scores
            most = scores[:, lanes[0]]
            for lane in lanes[1:]:
                most = jnp.maximum(most, scores[:, lane])
            top_ref[...] = jnp.maximum(top_ref[...], most)
            return 0
        lax.fori_loop(lo_tile, inner_lo, functools.partial(score, masked=True), 0)
        lax.fori_loop(inner_lo, inner_hi, functools.partial(score, masked=False), 0)
        lax.fori_loop(inner_hi, hi_tile, functools.partial(score, masked=True), 0)
        top_ref[...] = jnp.broadcast_to(jnp.max(top_ref[...], axis=1, keepdims=True), (rows, HEAD_DIM))
        total_ref[...] = jnp.zeros((rows, HEAD_DIM), jnp.float32)
        acc_ref[...] = jnp.zeros((rows, HEAD_DIM), jnp.float32)

        def weigh(t, _, kv_head=kv_head):
            at = pl.ds(pl.multiple_of(t * KEY_TILE, KEY_TILE), KEY_TILE)
            values = packed_kv[at, kv_cols + kv_head * HEAD_DIM:kv_cols + (kv_head + 1) * HEAD_DIM]
            top = top_ref[...]
            total, parts = (total_ref[...], [])
            for lane in lanes:
                part = jnp.exp2(score_ref[t - lo_tile, :, lane] - top)
                total = total + part
                parts.append(part.astype(jnp.bfloat16))
            total_ref[...] = total
            expo = jnp.concatenate(parts, axis=1)
            acc_ref[...] += jnp.dot(expo, values, preferred_element_type=jnp.float32)
            return 0
        lax.fori_loop(lo_tile, hi_tile, weigh, 0)
        heads = (acc_ref[...] / jnp.sum(total_ref[...], axis=1, keepdims=True)).astype(jnp.bfloat16)
        for h in range(group):
            to = (kv_head * group + h) * HEAD_DIM
            out_ref[:, to:to + HEAD_DIM] = heads[h * BLOCK:(h + 1) * BLOCK]

def attend(q, kv, rows_at, place, segment_ids, first=0):
    blocks = place.shape[0]
    tokens = segment_ids.shape[0]
    kv_heads = kv[0].shape[1] // (2 * HEAD_DIM)
    group = q.shape[1] // HEAD_DIM // kv_heads
    q_seg = segment_ids.reshape(-1, BLOCK)[place]
    doc_first = jnp.sum((segment_ids[None, :] < q_seg[:, :1]).astype(jnp.int32), axis=1)
    low = jnp.maximum(doc_first, place * BLOCK - (WINDOW - 1))
    last_first = jnp.sum((segment_ids[None, :] < q_seg[:, -1:]).astype(jnp.int32), axis=1)
    high = jnp.maximum(last_first, place * BLOCK + BLOCK - WINDOW)
    tiles = min(tokens // KEY_TILE, WINDOW // KEY_TILE + 2)
    rows = group * BLOCK
    grid = pltpu.PrefetchScalarGridSpec(num_scalar_prefetch=4, grid=(blocks,), in_specs=[pl.BlockSpec((BLOCK, q.shape[1]), lambda i, *_: (first + i, 0)), pl.BlockSpec((BLOCK, 1), lambda i, *_: (i, 0)), pl.BlockSpec((1, tokens), lambda i, *_: (0, 0))] + [pl.BlockSpec(part.shape, lambda i, *_: (0, 0)) for part in kv], out_specs=pl.BlockSpec((BLOCK, q.shape[1]), lambda i, *_: (i, 0)), scratch_shapes=[pltpu.VMEM((tokens, kv[0].shape[1]), jnp.bfloat16), pltpu.VMEM((tiles, rows, KEY_TILE), jnp.float32)] + [pltpu.VMEM((rows, HEAD_DIM), jnp.float32)] * 3)
    rows = blocks * BLOCK
    return pl.pallas_call(functools.partial(attention_kernel, group, kv_heads, len(kv)), grid_spec=grid, out_shape=jax.ShapeDtypeStruct((rows, q.shape[1]), jnp.bfloat16), compiler_params=pltpu.CompilerParams(vmem_limit_bytes=48 << 20), cost_estimate=pl.CostEstimate(flops=4 * rows * q.shape[1] * tokens // 2, bytes_accessed=4 * rows * q.shape[1] + 2 * tokens * kv[0].shape[1], transcendentals=rows * (q.shape[1] // HEAD_DIM) * tokens // 2), name='attend')(place, low, high, rows_at, q, q_seg.reshape(-1, 1), segment_ids.reshape(1, -1), *kv)

def product_kernel(layout, kinds, slots, *refs):
    out_ref = refs[-1]

    def write(w_ref):
        row = 0
        for h, adds in layout:
            total = jnp.dot(refs[h][...], w_ref[...], preferred_element_type=jnp.float32)
            for a in adds:
                total = total + refs[a][...].astype(jnp.float32)
            rows = total.shape[0]
            out_ref[row:row + rows, :] = total.astype(out_ref.dtype)
            row += rows
    if kinds == 1:
        write(refs[0])
    else:
        for k in range(kinds):
            pl.when(slots[0] == k)(functools.partial(write, refs[k]))

def product(parts, weight, slots, adds=None, tile=384, first=0, tiles=None):
    kinds = len(weight) if isinstance(weight, list) else 1
    depth, cols = (weight[0] if kinds > 1 else weight).shape[-2:]
    per_group = cols // tile
    tiles = tiles or per_group
    if kinds > 1:
        operands = list(weight)
        in_specs = [pl.BlockSpec((depth, tile), lambda g, j, s, k=k: (0, jnp.where(s[0] == k, first + j, first))) for k in range(kinds)]
    else:
        operands = [weight]
        in_specs = [pl.BlockSpec((None, depth, tile), lambda g, j, s: (s[g], 0, first + j))]
    layout = []
    for p, h in enumerate(parts):
        rows = h.shape[0]
        operands.append(h)
        in_specs.append(pl.BlockSpec((rows, depth), lambda g, j, s: (0, 0)))
        at, more = (len(operands) - 1, [])
        for a, r, slotted in adds[p] if adds else ():
            operands.append(a)
            if slotted:
                in_specs.append(pl.BlockSpec((rows, tile), lambda g, j, s, r=r: (r, s[g] * per_group + first + j)))
            else:
                in_specs.append(pl.BlockSpec((rows, tile), lambda g, j, s, r=r: (r, g * tiles + j)))
            more.append(len(operands) - 1)
        layout.append((at, more))
    rows = sum((h.shape[0] for h in parts))
    groups = slots.shape[0]
    return pl.pallas_call(functools.partial(product_kernel, layout, kinds), grid_spec=pltpu.PrefetchScalarGridSpec(num_scalar_prefetch=1, grid=(groups, tiles), in_specs=in_specs, out_specs=pl.BlockSpec((rows, tile), lambda g, j, s: (0, g * tiles + j))), out_shape=jax.ShapeDtypeStruct((rows, groups * tiles * tile), jnp.bfloat16), compiler_params=pltpu.CompilerParams(vmem_limit_bytes=40 << 20), cost_estimate=pl.CostEstimate(flops=int(1 * 2 * rows * depth * groups * tiles * tile), bytes_accessed=int(1 * (2 * depth * (rows + groups * tiles * tile) + 4 * rows * groups * tiles * tile)), transcendentals=0), name='product')(slots, *operands)

def pick_kernel(pools, source, *refs):
    outs = refs[pools:]
    per_out = outs[0].shape[0] // BLOCK
    for i in range(source.shape[0]):
        row = source[i] * BLOCK
        out = outs[i // per_out]
        to = slice(i % per_out * BLOCK, (i % per_out + 1) * BLOCK)
        low = 0
        for pool in refs[:pools]:

            @pl.when((row >= low) & (row < low + pool.shape[0]))
            def _(pool=pool, row=row, out=out, to=to, low=low):
                out[to, :] = pool[pl.ds(pl.multiple_of(row - low, BLOCK), BLOCK), :]
            low += pool.shape[0]

def pick_blocks(pools, cols, source, outs):
    rows = source.shape[0] * BLOCK // outs
    size = 2 * cols * (sum((p.shape[0] for p, _ in pools)) + rows * outs)
    return pl.pallas_call(functools.partial(pick_kernel, len(pools)), grid_spec=pltpu.PrefetchScalarGridSpec(num_scalar_prefetch=1, grid=(1,), in_specs=[pl.BlockSpec((p.shape[0], cols), lambda i, s, g=g: (0, g)) for p, g in pools], out_specs=[pl.BlockSpec((rows, cols), lambda i, s: (0, 0))] * outs), out_shape=[jax.ShapeDtypeStruct((rows, cols), jnp.bfloat16)] * outs, compiler_params=pltpu.CompilerParams(vmem_limit_bytes=40 << 20), cost_estimate=pl.CostEstimate(flops=0, bytes_accessed=size, transcendentals=0), name='pick_blocks')(source, *[p for p, _ in pools])

def sources_of(packing, per_shard):
    blocks = packing.shape[0]
    target = packing[:, 0] * per_shard + packing[:, 1]
    at = jnp.arange(blocks, dtype=jnp.int32)
    return (target, jnp.sum(jnp.where(target[None, :] == at[:, None], at[None, :], 0), axis=1))

def plain_plan(queries, keys, values, segment_ids, packing, out_weight):
    tok_rows = queries.shape[0]
    per_shard = tok_rows // BLOCK
    me = lax.axis_index('seq')
    target, source = sources_of(packing, per_shard)
    place = lax.dynamic_slice_in_dim(target, me * per_shard, per_shard, 0)
    kv = lax.all_gather(jnp.concatenate([keys, values], axis=1), 'seq', axis=0, tiled=True)
    heads = attend(queries, [kv], source * BLOCK, place, segment_ids)
    heads = lax.all_gather(heads, 'seq', axis=0, tiled=True)
    own = lax.dynamic_slice_in_dim(source, me * per_shard, per_shard, 0)
    heads = heads.reshape(-1, BLOCK, heads.shape[1])[own].reshape(tok_rows, -1)
    weight = lax.all_gather(out_weight, 'seq', axis=1, tiled=True)
    terms = jnp.dot(heads, weight, preferred_element_type=jnp.float32).astype(jnp.bfloat16)
    return lax.psum_scatter(terms, 'tp', scatter_dimension=1, tiled=True)

def after(array, *others):
    return lax.optimization_barrier((array, *others))[0]

def paired_plan(queries, keys, values, segment_ids, packing, out_weight):
    tok_rows, q_cols = queries.shape
    per_shard = tok_rows // BLOCK
    quarter = out_weight.shape[1] // 2
    half = quarter // 2
    me, z = (lax.axis_index('seq'), lax.axis_index('tp'))
    chip, core = (me // 2, me % 2)
    x, pair = (chip % 2, z // 2)
    target, source = sources_of(packing, per_shard)
    place = lax.dynamic_slice_in_dim(target, me * per_shard, per_shard, 0)

    def across(array, mask):
        return lax.ppermute(array, 'seq', [(i, i ^ mask) for i in range(8)])

    def along(array, *route):
        return lax.ppermute(array, 'tp', route)
    kv = jnp.concatenate([keys, values], axis=1)
    kv_x, kv_y, kv_d = (across(kv, 2), across(kv, 4), across(kv, 6))
    pieces = [lax.dynamic_slice_in_dim(out_weight, (x ^ flip) * quarter, quarter, 1) for flip in range(2)]
    kv_own = jnp.concatenate([kv, after(kv_x, *pieces), kv_y, kv_d], axis=0)
    kv_other = across(kv_own, 1)

    def row_of(block):
        relative = block // per_shard ^ me
        return ((relative >> 1) + 4 * (relative & 1)) * tok_rows + block % per_shard * BLOCK
    weights = []
    for flip, piece in enumerate(pieces):
        route = []
        for s in range(8):
            sy, sx, sa = (s // 4, s // 2 % 2, s % 2)
            d = 4 * sa + 2 * (sx ^ flip) + sy
            if s != d:
                route.append((s, d))
        weights.append(lax.ppermute(after(piece, kv_x, kv_y, kv_d), 'seq', route))
    stays = core == chip // 2
    twins = [(i, i ^ 1) for i in range(8) if i % 2 == i // 4]
    given = lax.ppermute(after(pieces[0], kv_other), 'seq', twins)
    heads = attend(queries, [kv_own, kv_other], row_of(source), place, segment_ids)
    mine = [heads, across(heads, 2), across(heads, 4)]
    here = core == pair
    flips = jnp.arange(2, dtype=jnp.int32)
    returned = lax.ppermute(after(weights[0], heads), 'seq', [(d, s) for s, d in twins])
    crossed = across(after(weights[1], heads), 1)
    kinds = [[pieces[0], weights[0], given, returned], [weights[1], crossed]]
    kind = [jnp.where(here, jnp.where(stays, 3, 2), jnp.where(stays, 0, 1)), here.astype(jnp.int32)]

    def settle(*others):
        own = [jnp.where(stays, pieces[0], after(weights[0], *others)), after(weights[1], *others)]
        other = [jnp.where(stays, after(returned, *others), given), after(crossed, *others)]
        far = jnp.stack([jnp.where(here, o, w) for w, o in zip(own, other)])
        return (far, (own, other))

    def add(a, b):
        return (a.astype(jnp.float32) + b.astype(jnp.float32)).astype(jnp.bfloat16)
    chunks = [(0, 0), (0, 1), (1, None), (2, None), (3, None)]
    last = len(chunks) - 1
    shares, inward = ([], [])
    sums, arrived = ([None] * len(chunks), [None] * len(chunks))

    def pass_on(i, *later):
        sums[i] = add(after(shares[i], *later) if later else shares[i], inward[i])
        arrived[i] = along(sums[i], (1, 2), (2, 1))
    both = None
    for i, (r, flip) in enumerate(chunks):
        if i == 2:
            mine.append(across(after(heads, shares[1], mine[1], mine[2]), 6))
            both, sides = settle(shares[1])
        rows = mine[r]
        if i == 1:
            rows = after(rows, shares[0])
        elif i:
            needs = [s for s in sums[:i - 1] if s is not None]
            needs += [a for a in arrived[:i - 2] if a is not None]
            rows = after(rows, shares[i - 1], *needs, *(mine[1:3] if i == 2 else ()))
        if i < 2:
            share = product([rows], kinds[i], kind[i][None])
        else:
            share = product([rows], both, flips if flip is None else flips[flip:flip + 1])
        shares.append(share)
        inward.append(along(share, (0, 1), (3, 2)))
        for j in range(i + 1):
            if sums[j] is None and j + (0, 0, 0, 1, 0, 0)[j] <= i and (j < last):
                pass_on(j, *([shares[i]] if i > j else []))
    own, other = sides
    near = jnp.stack([jnp.where(here, after(w, shares[-1]), o) for w, o in zip(own, other)])
    own_slot = (z & 1 ^ x).astype(jnp.int32)[None]
    came = [None] * 4

    def swap(r, first=0, tiles=2):
        share = product([mine[r]], near, 1 - own_slot, [[(came[r], 0, True)]], half, first, tiles)
        return (share, along(share, (0, 1), (1, 0), (2, 3), (3, 2)))

    def total(parts, swapped, first=0, tiles=2):
        adds = [[(came[r], 0, True), (some, 0, False)] for r, some in zip(parts, swapped)]
        return product([mine[r] for r in parts], near, own_slot, adds, half, first, tiles)
    for j in range(last):
        if sums[j] is None:
            pass_on(j, shares[-1])
    came[0] = jnp.concatenate(arrived[:2], axis=1)
    came[1], came[2] = (arrived[2], arrived[3])
    came[3] = None
    swapped, order_of = ({}, ((0, None), (1, None), (2, None), (3, 0), (3, 1)))
    share = None
    for r, h in order_of:
        tiles = 2 if h is None else 1
        if r == 3 and came[3] is None:
            pass_on(last)
            came[3] = arrived[4]
        share, some = swap(r, h or 0, tiles)
        swapped[r, h] = (share, some)
    split = (0, 0) in swapped
    late = [swapped[3, h][1] for h in range(2)]
    if split:
        early = [[swapped[r, h][1] for r in range(3)] for h in range(2)]
        done = [total((0, 1, 2), early[h], h, 1) for h in range(2)]
        done = [(d, across(d, 1)) for d in done]
    else:
        early = [swapped[r, None][1] for r in range(3)]
        done = total((0, 1, 2), early)
        done = [done, across(done, 1)]
    picks = []
    for r in range(4):
        blocks = lax.dynamic_slice_in_dim(source, (me ^ 2 * r) * per_shard, per_shard, 0)
        picks.append(row_of(blocks) // BLOCK)
    picks = jnp.concatenate(picks)
    result = jnp.zeros((tok_rows, 4 * quarter), jnp.bfloat16)
    for h in range(2):
        some = total((3,), [late[h]], h, 1)
        pools = [(d, 0) for d in done[h]] if split else [(d, h) for d in done]
        rows = pick_blocks([pools[0], (some, 0), pools[1], (across(some, 1), 0)], half, picks, 4)
        for r in range(4):
            some = across(rows[r], 2 * r) if r else rows[r]
            result = lax.dynamic_update_slice_in_dim(result, some, (chip ^ r) * quarter + h * half, 1)
    return result

def solution(mesh):
    in_specs = (P('seq', 'tp'), P('seq', 'tp'), P('seq', 'tp'), P(), P(), P('tp', 'seq'))
    out_specs = P('seq', 'tp')
    paired = mesh.shape['seq'] == 8 and mesh.shape['tp'] == 4
    shards = paired_plan if paired else plain_plan
    return jax.shard_map(shards, mesh=mesh, in_specs=in_specs, out_specs=out_specs, check_vma=False)
```
